32 devices in a mesh: dev: 32 (over z, y, x, core).
Axes of the slice: x: 2, y: 2, z: 4, core: 2. Of those that a mesh axis runs over, the one named last changes fastest.
Arguments:
- tokens: bfloat16 [65536, 768], P('dev'), may hold values from -6 to 6
- cotangent: bfloat16 [65536, 768], P('dev'), may hold values from -6 to 6
- in_weight: bfloat16 [768, 3352], P('dev'), may hold values from -0.21875 to 0.21875
- out_weight: bfloat16 [1536, 768], P('dev'), may hold values from -0.3125 to 0.3125
- conv_weight: bfloat16 [1792, 4], P('dev'), may hold values from -3 to 3
- conv_bias: bfloat16 [1792], P('dev'), may hold values from -3 to 3
- norm_gain: bfloat16 [768], P('dev'), may hold values from 0.5 to 1.5
- gated_gain: bfloat16 [1536], P('dev'), may hold values from 0.5 to 1.5
- head_params: float32 [3, 24], replicated, may hold values from -7 to 3, as said below
- group_length: int32 [256], P('dev'), may hold values from 0 to 256, as said below
- group_first: int32 [256], P('dev'), may hold values from 0 to 1, as said below
Outputs:
- block_out: bfloat16 [65536, 768], P('dev')
- token_grad: float32 [65536, 768], P('dev')
- in_weight_grad: float32 [768, 3352], P('dev')
- out_weight_grad: float32 [1536, 768], P('dev')
- conv_weight_grad: float32 [1792, 4], P('dev')
- conv_bias_grad: float32 [1792], P('dev')
- norm_gain_grad: float32 [768], P('dev')
- gated_gain_grad: float32 [1536], P('dev')
- head_grad: float32 [3, 24], replicated
The draws below stay inside these ranges and needn't reach their ends.
Inputs may be any that keep to these rules, and one draw needn't show every extreme that they name: `head_params`: step bias per head between inverse softplus of 0.001 and of 0.1; log decay between 0 and log 16; skip factor between 0.5 and 1.5. `group_length`: each device's first group is full. A group's live tokens come first in it. `group_first`: A sequence spans one or two groups of one device; a continuing group stands at an odd group place of its device, follows a full group, and has live tokens. Each device's first group begins a sequence.
All inputs are finite; a program needn't handle non-finite values.
Results may differ from the reference program's by a relative error of at most 0.007.
Values may be sent and summed in bfloat16 or wider, within the bound.
A program may use at most 384 MiB of HBM per device.

```python
import math
import jax
import jax.numpy as jnp
from jax import lax

D = 768
HEADS = 24
HEAD_DIM = 64
STATE = 128
KERNEL = 4
GROUP = 256
GROUP_DEV = 8
INNER = 1536
CONV_CH = 1792
PROJ = 3352
TOKENS = 65536
TOTAL_GROUPS = 256


def group_layout(key):
    keys = jax.random.split(key, 4)
    index = jnp.arange(TOTAL_GROUPS, dtype=jnp.int32)
    place = index % GROUP_DEV
    raw = jax.random.randint(keys[0], (TOTAL_GROUPS,), 1, GROUP + 1)
    full = jax.random.randint(keys[1], (TOTAL_GROUPS,), 0, 2) == 1
    empty = jax.random.randint(keys[2], (TOTAL_GROUPS,), 0, 4) == 0
    length = jnp.where(full, GROUP, raw)
    length = jnp.where(empty & (place > 0), 0, length)
    length = jnp.where(place == 0, GROUP, length)
    coin = jax.random.randint(keys[3], (TOTAL_GROUPS,), 0, 2) == 1
    previous = jnp.concatenate([jnp.zeros((1,), jnp.int32), length[:-1]])
    continues = (place % 2 == 1) & (previous == GROUP) & coin & (length > 0)
    first = jnp.where(continues, 0, 1).astype(jnp.int32)
    return (length.astype(jnp.int32), first)


def draw_group_length(key, part):
    length, first = group_layout(key)
    return length


def draw_group_first(key, part):
    length, first = group_layout(key)
    return first


def draw_head_params(key, part):
    key = jax.random.fold_in(key, 5)
    keys = jax.random.split(key, 3)
    decay_log = jnp.log(jax.random.uniform(keys[0], (HEADS,), jnp.float32, 1.0, 16.0))
    skip_factor = jax.random.uniform(keys[1], (HEADS,), jnp.float32, 0.5, 1.5)
    step_value = jnp.exp(jax.random.uniform(keys[2], (HEADS,), jnp.float32, math.log(0.001), math.log(0.1)))
    step_bias = step_value + jnp.log(-jnp.expm1(-step_value))
    return jnp.stack([decay_log, skip_factor, step_bias]).astype(jnp.float32)


def block_scale(key, dims, cuts, smallest, largest):
    factor_of = 1.0
    for position, parts in cuts:
        steps = jax.random.uniform(jax.random.fold_in(jax.random.fold_in(key, 6), position), (parts,), jnp.float32, smallest / len(cuts), largest / len(cuts))
        factor_of = factor_of * jnp.repeat(jnp.exp(steps), dims[position] // parts).reshape((-1,) + (1,) * (len(dims) - 1 - position))
    return factor_of


def scatter_about(rng, shape, scale, reach, cuts=(), kind=jnp.bfloat16):
    loudness = block_scale(rng, shape, cuts, -0.22, 0.18) if cuts else 1.0
    values = jax.random.normal(rng, shape, jnp.float32) * scale * loudness
    return jnp.minimum(jnp.maximum(values, -reach), reach).astype(kind)


def setup_inputs(seed: int = 0) -> dict:
    seeds = jax.random.split(jax.random.key(seed), 12)
    return {
        "tokens": scatter_about(seeds[0], (TOKENS, D), 1.0, 6.0, ((0, 32),)),
        "cotangent": scatter_about(seeds[1], (TOKENS, D), 1.0, 6.0, ((0, 32),)),
        "in_weight": scatter_about(seeds[2], (D, PROJ), D ** -0.5, 0.21875, ((0, 32),)),
        "out_weight": scatter_about(seeds[3], (INNER, D), (INNER // 4) ** -0.5, 0.3125, ((0, 32),)),
        "conv_weight": scatter_about(seeds[4], (CONV_CH, KERNEL), KERNEL ** -0.5, 3.0, ((0, 32),)),
        "conv_bias": scatter_about(seeds[5], (CONV_CH,), 0.5, 3.0, ((0, 32),)),
        "norm_gain": jnp.clip(1.0 + 0.1 * jax.random.normal(seeds[6], (D,), jnp.float32), 0.5, 1.5).astype(jnp.bfloat16),
        "gated_gain": jnp.clip(1.0 + 0.1 * jax.random.normal(seeds[7], (INNER,), jnp.float32), 0.5, 1.5).astype(jnp.bfloat16),
        "head_params": draw_head_params(jax.random.fold_in(seeds[11], 71), 0),
        "group_length": draw_group_length(jax.random.fold_in(seeds[11], 71), 0),
        "group_first": draw_group_first(jax.random.fold_in(seeds[11], 71), 0),
    }


@jax.custom_vjp
def low(v):
    return lax.optimization_barrier(v.astype(jnp.bfloat16)).astype(jnp.float32)

@jax.custom_vjp
def low_back(v):
    return v

def low_keep(v):
    return (low(v), None)

def low_pass(kept, grad):
    return (grad,)

def back_keep(v):
    return (v, None)

def back_low(kept, grad):
    return (low(grad),)
low.defvjp(low_keep, low_pass)
low_back.defvjp(back_keep, back_low)
EPSILON = 1e-05

def exact_dot(left, right):
    return jnp.dot(left, right, precision=lax.Precision.HIGHEST)

def group_mixer(decay_rate):

    def advance(state, pieces):
        c_rows, b_rows, x_heads, step_size, carry_on = pieces
        running = jnp.cumsum(step_size * decay_rate[None, :], axis=0)
        places = jnp.arange(c_rows.shape[0])
        causal = (places[:, None] >= places[None, :])[:, :, None]
        spread = running[:, None, :] - running[None, :, :]
        decay = jnp.where(causal, jnp.exp(jnp.where(causal, spread, 0.0)), 0.0)
        scores = exact_dot(c_rows, b_rows.T)
        mixing = low(jnp.transpose(scores[:, :, None] * decay * step_size[None, :, :], (2, 0, 1)))
        inner = jnp.einsum('hts,shp->thp', mixing, x_heads, precision=lax.Precision.HIGHEST)
        start = state * carry_on
        outer = jnp.exp(running)[:, :, None] * jnp.einsum('tn,hnp->thp', c_rows, low(start), precision=lax.Precision.HIGHEST)
        to_end = jnp.exp(running[-1][None, :] - running) * step_size
        weighted = low(x_heads * to_end[:, :, None])
        fresh = jnp.einsum('sn,shp->hnp', b_rows, weighted, precision=lax.Precision.HIGHEST)
        new_state = jnp.exp(running[-1])[:, None, None] * start + fresh
        return (new_state, inner + outer)
    return advance

def block_forward(tokens, in_w, out_w, conv_w, conv_b, norm_g, gated_g, head_p, lengths, firsts):
    total_rows = tokens.shape[0]
    group_count = total_rows // GROUP
    place = jnp.arange(total_rows, dtype=jnp.int32) % GROUP
    live = (place < jnp.repeat(lengths, GROUP)).astype(jnp.float32)
    seq_place = place + GROUP * (1 - jnp.repeat(firsts, GROUP))
    normed = tokens * lax.rsqrt(lax.optimization_barrier(jnp.mean(tokens * tokens, axis=1, keepdims=True)) + EPSILON) * norm_g
    projected = low_back(exact_dot(low(normed), in_w))
    gate_part = projected[:, :INNER]
    conv_in = projected[:, INNER:INNER + CONV_CH]
    raw_step = projected[:, INNER + CONV_CH:]
    mixed_conv = conv_b + conv_in * conv_w[:, KERNEL - 1]
    for lag in range(1, KERNEL):
        earlier = jnp.concatenate([jnp.zeros((lag, CONV_CH), jnp.float32), conv_in[:-lag]], axis=0)
        keep = (seq_place >= lag).astype(jnp.float32)[:, None]
        mixed_conv = mixed_conv + conv_w[:, KERNEL - 1 - lag] * earlier * keep
    activated = low(jax.nn.silu(mixed_conv))
    x_heads = activated[:, :INNER].reshape(total_rows, HEADS, HEAD_DIM)
    b_rows = activated[:, INNER:INNER + STATE]
    c_rows = activated[:, INNER + STATE:]
    step_size = jax.nn.softplus(raw_step + head_p[2][None, :])
    decay_rate = -jnp.exp(head_p[0])
    carry_on = (1 - firsts).astype(jnp.float32)
    pieces = (c_rows.reshape(group_count, GROUP, STATE), b_rows.reshape(group_count, GROUP, STATE), x_heads.reshape(group_count, GROUP, HEADS, HEAD_DIM), step_size.reshape(group_count, GROUP, HEADS), carry_on)
    initial = jnp.zeros((HEADS, STATE, HEAD_DIM), jnp.float32)
    final_state, mixer = lax.scan(jax.checkpoint(group_mixer(decay_rate)), initial, pieces)
    mixer = mixer.reshape(total_rows, HEADS, HEAD_DIM) + head_p[1][None, :, None] * x_heads
    gated = mixer.reshape(total_rows, INNER) * jax.nn.silu(gate_part)
    gnormed = gated * lax.rsqrt(lax.optimization_barrier(jnp.mean(gated * gated, axis=1, keepdims=True)) + EPSILON) * gated_g
    branch = exact_dot(low(gnormed), out_w)
    return tokens + live[:, None] * branch

def reference(tokens, cotangent, in_weight, out_weight, conv_weight, conv_bias, norm_gain, gated_gain, head_params, group_length, group_first):
    floats = (tokens.astype(jnp.float32), in_weight.astype(jnp.float32), out_weight.astype(jnp.float32), conv_weight.astype(jnp.float32), conv_bias.astype(jnp.float32), norm_gain.astype(jnp.float32), gated_gain.astype(jnp.float32), head_params.astype(jnp.float32))

    def forward(tok, in_w, out_w, conv_w, conv_b, norm_g, gated_g, head_p):
        return block_forward(tok, in_w, out_w, conv_w, conv_b, norm_g, gated_g, head_p, group_length, group_first)
    result, pullback = jax.vjp(forward, *floats)
    grads = pullback(cotangent.astype(jnp.float32))
    return (result.astype(jnp.bfloat16), grads[0], grads[1], grads[2], grads[3], grads[4], grads[5], grads[6], grads[7])
```

```python
import jax
import jax.numpy as jnp
from jax import lax
from jax.experimental import pallas as pl
from jax.experimental.pallas import tpu as pltpu
from jax.sharding import PartitionSpec as P

HEADS = 24
HEAD_DIM = 64
STATE = 128
KERNEL = 4
GROUP = 256
INNER = 1536
CONV_CH = 1792
D = 768
PROJ = 3352
PAIR = 2 * GROUP
LANES = 128
CHUNKS = INNER // LANES
EPSILON = 1e-05
LOG2E = 1.4426950408889634
F32 = jnp.float32
BF16 = jnp.bfloat16


def mm(left, right, dims=((1,), (0,))):
    return lax.dot_general(left, right, (dims, ((), ())), preferred_element_type=F32)


def exact(left, right):
    return jnp.dot(left, right, precision=lax.Precision.HIGHEST, preferred_element_type=F32)


NT = ((1,), (1,))
TN = ((0,), (0,))


def pair_kernel(
    len_ref, first_ref, proj_ref, raw_ref, tok_ref, cot_ref, outw_ref, cw_ref, cb_ref, gg_ref, heads_ref, skip_ref,
    blk_ref, gn_ref, dproj_ref, dcw_ref, dcb_ref, dgg_ref, dskip_ref, dhead_ref,
    dg_s, y_s, m_s, x_s, b_s, c_s, start_s, s_s, ds_s, db_s, dc_s, at_s, run_s, dt_s, da_s, ddt_s, tot_s,
):
    pair = pl.program_id(0)
    cont = (1 - first_ref[2 * pair + 1]).astype(F32)
    row = lax.broadcasted_iota(jnp.int32, (PAIR, LANES), 0)
    lane = lax.broadcasted_iota(jnp.int32, (PAIR, LANES), 1)
    low_half = lane < HEAD_DIM
    low_g = low_half[:GROUP]
    place = jnp.where(row >= GROUP, row - GROUP, row)
    open_row = jnp.where(row >= GROUP, cont, 0.0)
    tri_t = lax.broadcasted_iota(jnp.int32, (GROUP, GROUP), 0)
    tri_s = lax.broadcasted_iota(jnp.int32, (GROUP, GROUP), 1)
    causal = tri_s <= tri_t

    @pl.when(pair == 0)
    def _():
        dcw_ref[...] = jnp.zeros_like(dcw_ref)
        dcb_ref[...] = jnp.zeros_like(dcb_ref)
        dgg_ref[...] = jnp.zeros_like(dgg_ref)
        dskip_ref[...] = jnp.zeros_like(dskip_ref)
        dhead_ref[...] = jnp.zeros_like(dhead_ref)

    def keep(lag):
        return jnp.where(place >= lag, 1.0, open_row)

    row1 = lax.broadcasted_iota(jnp.int32, (PAIR, 1), 0)
    limit = jnp.where(row1 >= GROUP, len_ref[2 * pair + 1], len_ref[2 * pair])
    live = jnp.where(jnp.where(row1 >= GROUP, row1 - GROUP, row1) < limit, 1.0, 0.0)

    picked = (cot_ref[...].astype(F32) * live).astype(BF16)
    for piece in range(4):
        part = pl.ds(piece * 384, 384)
        dg_s[:, part] = mm(picked, outw_ref[part, :], NT)

    biased = raw_ref[...] + heads_ref[2:3, :]
    small = jnp.exp(-jnp.abs(biased))
    step = jnp.maximum(biased, 0.0) + jnp.where(small < 1e-3, small * (1.0 - 0.5 * small), jnp.log(1.0 + small))
    rate = -jnp.exp(heads_ref[0:1, :])
    log_decay = step * rate
    lower = jnp.where(causal, 1.0, 0.0)
    upper = jnp.where(tri_s >= tri_t, 1.0, 0.0)
    for g in range(2):
        rows = slice(g * GROUP, (g + 1) * GROUP)
        run_s[rows, :] = exact(lower, log_decay[rows]) * LOG2E
    dt_s[...] = step
    at_s[...] = run_s[...].T

    def taps(columns):
        return cw_ref[:, columns], cb_ref[:, columns]

    def conv(j):
        cin = proj_ref[:, pl.ds(pl.multiple_of(INNER + j * LANES, LANES), LANES)]
        columns = pl.ds(pl.multiple_of(j * LANES, LANES), LANES)
        weight, bias = taps(columns)
        mixed = bias + cin * weight[KERNEL - 1 : KERNEL]
        for lag in range(1, KERNEL):
            mixed = mixed + weight[KERNEL - 1 - lag : KERNEL - lag] * (pltpu.roll(cin, lag, 0) * keep(lag))
        m_s[:, columns] = mixed
        return (mixed / (1.0 + jnp.exp(-mixed))).astype(BF16)

    def conv_back(j, grad):
        columns = pl.ds(pl.multiple_of(j * LANES, LANES), LANES)
        place_in = pl.ds(pl.multiple_of(INNER + j * LANES, LANES), LANES)
        weight, _ = taps(columns)
        mixed = m_s[:, columns]
        cin = proj_ref[:, place_in]
        sig = 1.0 / (1.0 + jnp.exp(-mixed))
        dm = grad * (sig * (1.0 + mixed * (1.0 - sig)))
        dcb_ref[:, columns] += jnp.sum(dm, axis=0, keepdims=True)
        total = dm * weight[KERNEL - 1 : KERNEL]
        dws = [jnp.sum(dm * cin, axis=0, keepdims=True)]
        for lag in range(1, KERNEL):
            kept = dm * keep(lag)
            dws.append(jnp.sum(kept * pltpu.roll(cin, lag, 0), axis=0, keepdims=True))
            total = total + pltpu.roll(kept, PAIR - lag, 0) * weight[KERNEL - 1 - lag : KERNEL - lag]
        dcw_ref[:, columns] += jnp.concatenate(dws[::-1], axis=0)
        dproj_ref[:, place_in] = total.astype(BF16)

    b_s[...] = conv(CHUNKS)
    c_s[...] = conv(CHUNKS + 1)
    for g in range(2):
        rows = slice(g * GROUP, (g + 1) * GROUP)
        s_s[g] = jnp.where(causal, mm(c_s[rows, :], b_s[rows, :], NT), 0.0)
        ds_s[g] = jnp.zeros((GROUP, GROUP), F32)
    db_s[...] = jnp.zeros_like(db_s)
    dc_s[...] = jnp.zeros_like(dc_s)
    da_s[...] = jnp.zeros_like(da_s)
    ddt_s[...] = jnp.zeros_like(ddt_s)
    tot_s[...] = jnp.zeros_like(tot_s)

    def column(table, h):
        return jnp.sum(jnp.where(lane == h, table, 0.0), axis=1, keepdims=True)

    def head_columns(hp):
        run, dt = run_s[...], dt_s[...]
        runs = (column(run, 2 * hp), column(run, 2 * hp + 1))
        dts = jnp.where(low_half, column(dt, 2 * hp), column(dt, 2 * hp + 1))
        return runs, jnp.where(low_half, runs[0], runs[1]), dts

    def decay(runs, hp, g, k):
        rows = slice(g * GROUP, (g + 1) * GROUP)
        across = at_s[pl.ds(2 * hp + k, 1), rows]
        return jnp.exp2(jnp.minimum(runs[k][rows] - across, 0.0))

    def to_end(wide):
        return jnp.exp2(wide[GROUP - 1 : GROUP] - wide[:GROUP])

    def forward(hp, sums):
        square, cross = sums
        columns = pl.ds(pl.multiple_of(hp * LANES, LANES), LANES)
        x_low = conv(hp)
        x_s[:, columns] = x_low
        x = x_low.astype(F32)
        runs, wide, dts = head_columns(hp)
        xdt = (x * dts).astype(BF16)
        weighted = (x[:GROUP] * (to_end(wide) * dts[:GROUP])).astype(BF16)
        start = (mm(b_s[:GROUP, :], weighted, TN) * cont).astype(BF16)
        start_s[:, columns] = start
        inner = []
        for g in range(2):
            rows = slice(g * GROUP, (g + 1) * GROUP)
            halves = [mm((s_s[g] * decay(runs, hp, g, k)).astype(BF16), xdt[rows]) for k in range(2)]
            inner.append(jnp.where(low_g, halves[0], halves[1]))
        inner[1] = inner[1] + jnp.exp2(wide[GROUP:]) * mm(c_s[GROUP:, :], start)
        y = jnp.concatenate(inner, axis=0)
        y_s[:, columns] = y
        gate = proj_ref[:, columns]
        gated = (y + skip_ref[:, columns] * x) * (gate / (1.0 + jnp.exp(-gate)))
        return (square + gated * gated, cross + dg_s[:, columns] * gg_ref[:, columns] * gated)

    zero = jnp.zeros((PAIR, LANES), F32)
    square, cross = lax.fori_loop(0, CHUNKS, forward, (zero, zero))
    scale = lax.rsqrt(jnp.sum(square, axis=1, keepdims=True) * (1.0 / INNER) + EPSILON)
    pull = scale * scale * scale * (jnp.sum(cross, axis=1, keepdims=True) * (1.0 / INNER))

    def put(h, value):
        return jnp.where(lane[: value.shape[0]] == h, value, 0.0)

    def head_sums(hp, value):
        first = jnp.sum(jnp.where(low_half[: value.shape[0]], value, 0.0), axis=1, keepdims=True)
        second = jnp.sum(jnp.where(low_half[: value.shape[0]], 0.0, value), axis=1, keepdims=True)
        return put(2 * hp, first) + put(2 * hp + 1, second)

    def backward(hp, carry):
        columns = pl.ds(pl.multiple_of(hp * LANES, LANES), LANES)
        x = x_s[:, columns].astype(F32)
        y = y_s[:, columns]
        skip = skip_ref[:, columns]
        mixer = y + skip * x
        gate = proj_ref[:, columns]
        sig = 1.0 / (1.0 + jnp.exp(-gate))
        act = gate * sig
        gated = mixer * act
        gain = gg_ref[:, columns]
        dgn = dg_s[:, columns]
        unit = gated * scale
        gn_ref[:, columns] = (unit * gain).astype(BF16)
        dgg_ref[:, columns] += jnp.sum(dgn * unit, axis=0, keepdims=True)
        dgated = dgn * gain * scale - gated * pull
        dproj_ref[:, columns] = (dgated * mixer * (sig * (1.0 + gate * (1.0 - sig)))).astype(BF16)
        dy = dgated * act
        dskip_ref[:, columns] += jnp.sum(dy * x, axis=0, keepdims=True)
        dy_low = dy.astype(BF16)
        dyr = dy_low.astype(F32)
        runs, wide, dts = head_columns(hp)
        xdt = (x * dts).astype(BF16)
        dxdt = []
        for g in range(2):
            rows = slice(g * GROUP, (g + 1) * GROUP)
            parts = []
            extra = jnp.zeros((GROUP, GROUP), F32)
            dy_g = dy_low[rows]
            for k in range(2):
                fade = decay(runs, hp, g, k)
                parts.append(mm((s_s[g] * fade).astype(BF16), dy_g, TN))
                mine = jnp.where(low_g if k == 0 else ~low_g, dyr[rows], 0.0).astype(BF16)
                extra = extra + mm(mine, xdt[rows], NT) * fade
            ds_s[g] += extra
            dxdt.append(jnp.where(low_g, parts[0], parts[1]))
        dxdt = jnp.concatenate(dxdt, axis=0)
        start = start_s[:, columns]
        lifted = (dyr[GROUP:] * jnp.exp2(wide[GROUP:])).astype(BF16)
        dc_s[GROUP:, :] += mm(lifted, start, NT)
        dstate = (mm(c_s[GROUP:, :], lifted, TN) * cont).astype(BF16)
        fade_end = to_end(wide)
        weight_end = fade_end * dts[:GROUP]
        weighted = (x[:GROUP] * weight_end).astype(BF16)
        db_s[:GROUP, :] += mm(weighted, dstate, NT)
        dweighted = mm(b_s[:GROUP, :], dstate)
        through = x[:GROUP] * dweighted
        spent = through * weight_end
        da = dyr * y - xdt.astype(F32) * dxdt
        ddt = x * dxdt
        da = jnp.concatenate([da[:GROUP] - spent, da[GROUP:]], axis=0)
        ddt = jnp.concatenate([ddt[:GROUP] + through * fade_end, ddt[GROUP:]], axis=0)
        da_s[...] += head_sums(hp, da)
        ddt_s[...] += head_sums(hp, ddt)
        tot_s[...] += head_sums(hp, jnp.broadcast_to(jnp.sum(spent, axis=0, keepdims=True), (8, LANES)))
        dx = dy * skip + dxdt * dts
        dx = jnp.concatenate([dx[:GROUP] + dweighted * weight_end, dx[GROUP:]], axis=0)
        conv_back(hp, dx)
        return carry

    lax.fori_loop(0, CHUNKS, backward, 0)

    for g in range(2):
        rows = slice(g * GROUP, (g + 1) * GROUP)
        dscore = jnp.where(causal, ds_s[g], 0.0).astype(BF16)
        dc_s[rows, :] += mm(dscore, b_s[rows, :])
        db_s[rows, :] += mm(dscore, c_s[rows, :], TN)
    conv_back(CHUNKS, db_s[...])
    conv_back(CHUNKS + 1, dc_s[...])

    dlog = []
    for g in range(2):
        rows = slice(g * GROUP, (g + 1) * GROUP)
        part = exact(upper, da_s[rows, :])
        dlog.append(part + tot_s[0:1, :] if g == 0 else part)
    dlog = jnp.concatenate(dlog, axis=0)
    step = dt_s[...]
    dstep = ddt_s[...] + dlog * rate
    draw = dstep / (1.0 + jnp.exp(-biased))
    dproj_ref[:, PROJ - HEADS : PROJ] = draw[:, :HEADS].astype(BF16)
    dhead_ref[0:1, :] += jnp.sum(dlog * step, axis=0, keepdims=True) * rate
    dhead_ref[2:3, :] += jnp.sum(draw, axis=0, keepdims=True)

    branch = mm(gn_ref[...], outw_ref[...])
    blk_ref[...] = (tok_ref[...].astype(F32) + live * branch).astype(BF16)


def run_pairs(lengths, firsts, projected, raw, tokens, cotangent, out_w, cw, cb, gg, heads, skip):
    rows = tokens.shape[0]

    def rowwise(width):
        return pl.BlockSpec((PAIR, width), lambda i: (i, 0))

    smem = pl.BlockSpec(memory_space=pltpu.SMEM)
    whole = pl.BlockSpec(memory_space=pltpu.VMEM)
    shape = jax.ShapeDtypeStruct
    return pl.pallas_call(
        pair_kernel,
        grid=(rows // PAIR,),
        in_specs=[smem, smem, rowwise(PROJ), rowwise(LANES), rowwise(D), rowwise(D)] + [whole] * 6,
        out_specs=[rowwise(D), rowwise(INNER), rowwise(PROJ)] + [whole] * 5,
        out_shape=[
            shape((rows, D), BF16),
            shape((rows, INNER), BF16),
            shape((rows, PROJ), BF16),
            shape((KERNEL, CONV_CH), F32),
            shape((1, CONV_CH), F32),
            shape((1, INNER), F32),
            shape((1, INNER), F32),
            shape((8, LANES), F32),
        ],
        scratch_shapes=[
            pltpu.VMEM((PAIR, INNER), F32),
            pltpu.VMEM((PAIR, INNER), F32),
            pltpu.VMEM((PAIR, CONV_CH), F32),
            pltpu.VMEM((PAIR, INNER), BF16),
            pltpu.VMEM((PAIR, LANES), BF16),
            pltpu.VMEM((PAIR, LANES), BF16),
            pltpu.VMEM((STATE, INNER), BF16),
            pltpu.VMEM((2, GROUP, GROUP), F32),
            pltpu.VMEM((2, GROUP, GROUP), F32),
            pltpu.VMEM((PAIR, LANES), F32),
            pltpu.VMEM((PAIR, LANES), F32),
            pltpu.VMEM((LANES, PAIR), F32),
            pltpu.VMEM((PAIR, LANES), F32),
            pltpu.VMEM((PAIR, LANES), F32),
            pltpu.VMEM((PAIR, LANES), F32),
            pltpu.VMEM((PAIR, LANES), F32),
            pltpu.VMEM((8, LANES), F32),
        ],
        compiler_params=pltpu.CompilerParams(
            dimension_semantics=("arbitrary",), vmem_limit_bytes=60 * 1024 * 1024
        ),
    )(lengths, firsts, projected, raw, tokens, cotangent, out_w, cw, cb, gg, heads, skip)


def body(
    tokens,
    cotangent,
    in_weight,
    out_weight,
    conv_weight,
    conv_bias,
    norm_gain,
    gated_gain,
    head_params,
    group_length,
    group_first,
):
    sizes = (conv_weight.size, conv_bias.size, norm_gain.size, gated_gain.size)
    cuts = (sizes[0], sizes[0] + sizes[1], sizes[0] + sizes[1] + sizes[2])
    packed = jnp.concatenate([conv_weight.reshape(-1), conv_bias, norm_gain, gated_gain])
    packed = lax.all_gather(packed[None], "dev", axis=0, tiled=True).astype(F32)
    conv_w, conv_b, norm_g, gated_g = jnp.split(packed, cuts, axis=1)
    conv_w = conv_w.reshape(CONV_CH, KERNEL).T
    conv_b, norm_g, gated_g = conv_b.reshape(1, -1), norm_g.reshape(1, -1), gated_g.reshape(1, -1)
    in_w = lax.all_gather(in_weight, "dev", axis=0, tiled=True)
    out_w = lax.all_gather(out_weight, "dev", axis=0, tiled=True)
    ndev = packed.shape[0]

    token_float = tokens.astype(F32)
    inv = lax.rsqrt(jnp.mean(token_float * token_float, axis=1, keepdims=True) + EPSILON)
    normed_low = (token_float * inv * norm_g).astype(BF16)
    projected = jnp.dot(normed_low, in_w, preferred_element_type=F32)
    raw = jnp.pad(projected[:, PROJ - HEADS :], ((0, 0), (0, LANES - HEADS)))
    heads = jnp.pad(head_params, ((0, 5), (0, LANES - HEADS)))
    skip = jnp.repeat(head_params[1], HEAD_DIM)[None, :]
    block_out, gnormed_low, grad_proj, dcw, dcb, dgg, dskip, dhead = run_pairs(
        group_length, group_first, projected, raw, tokens, cotangent, out_w, conv_w, conv_b, gated_g, heads, skip
    )

    rows = tokens.shape[0]
    slot_place = jnp.arange(rows, dtype=jnp.int32) % GROUP
    live_mask = (slot_place < jnp.repeat(group_length, GROUP)).astype(BF16)[:, None]
    picked = cotangent * live_mask
    out_grad = jnp.dot(gnormed_low.T, picked, preferred_element_type=F32)
    out_grad = lax.psum_scatter(out_grad, "dev", scatter_dimension=0, tiled=True)
    in_grad = jnp.dot(normed_low.T, grad_proj, preferred_element_type=F32)
    in_grad = lax.psum_scatter(in_grad, "dev", scatter_dimension=0, tiled=True)
    grad_normed = jnp.dot(grad_proj, in_w.T, preferred_element_type=F32)
    unit = token_float * inv
    grad_norm_g = jnp.sum(grad_normed * unit, axis=0)
    scaled = grad_normed * norm_g
    grad_tokens = inv * (scaled - unit * jnp.mean(scaled * unit, axis=1, keepdims=True))
    token_grad = cotangent.astype(F32) + grad_tokens

    small = jnp.concatenate(
        [
            dcw.T.reshape(ndev, -1),
            dcb.reshape(ndev, -1),
            grad_norm_g.reshape(ndev, -1),
            dgg.reshape(ndev, -1),
        ],
        axis=1,
    )
    width = small.shape[1]
    head_part = jnp.stack([dhead[0, :HEADS], jnp.sum(dskip.reshape(HEADS, HEAD_DIM), axis=1), dhead[2, :HEADS]])
    total = lax.psum(jnp.concatenate([small.reshape(-1), head_part.reshape(-1)]), "dev")
    head_total = total[ndev * width :].reshape(3, HEADS)
    mine = lax.dynamic_slice(total, (lax.axis_index("dev") * width,), (width,))
    cw_o, cb_o, ng_o, gg_o = jnp.split(mine, cuts)
    return (
        block_out,
        token_grad,
        in_grad,
        out_grad,
        cw_o.reshape(conv_weight.shape),
        cb_o,
        ng_o,
        gg_o,
        head_total,
    )


def solution(mesh):
    placed = (
        P("dev", None),
        P("dev", None),
        P("dev", None),
        P("dev", None),
        P("dev", None),
        P("dev"),
        P("dev"),
        P("dev"),
        P(),
        P("dev"),
        P("dev"),
    )
    return jax.shard_map(
        body,
        mesh=mesh,
        in_specs=placed,
        out_specs=(
            P("dev", None),
            P("dev", None),
            P("dev", None),
            P("dev", None),
            P("dev", None),
            P("dev"),
            P("dev"),
            P("dev"),
            P(),
        ),
        check_vma=False,
    )
```

```python
import jax
import jax.numpy as jnp
from jax import lax
from jax.experimental import pallas as pl
from jax.experimental.pallas import tpu as pltpu
from jax.sharding import PartitionSpec as P

HEADS = 24
HEAD_DIM = 64
STATE = 128
KERNEL = 4
GROUP = 256
INNER = 1536
CONV_CH = 1792
D = 768
PROJ = 3352
PAIR = 2 * GROUP
LANES = 128
CHUNKS = INNER // LANES
EPSILON = 1e-05
LOG2E = 1.4426950408889634
F32 = jnp.float32
BF16 = jnp.bfloat16


def mm(left, right, dims=((1,), (0,))):
    return lax.dot_general(left, right, (dims, ((), ())), preferred_element_type=F32)


def exact(left, right):
    return jnp.dot(left, right, precision=lax.Precision.HIGHEST, preferred_element_type=F32)


NT = ((1,), (1,))
TN = ((0,), (0,))


def pair_kernel(
    len_ref, first_ref, proj_ref, raw_ref, tok_ref, cot_ref, outw_ref, cw_ref, cb_ref, gg_ref, heads_ref, skip_ref,
    blk_ref, gn_ref, dproj_ref, dcw_ref, dcb_ref, dgg_ref, dskip_ref, dhead_ref,
    dg_s, y_s, m_s, x_s, b_s, c_s, start_s, s_s, ds_s, db_s, dc_s, at_s, run_s, dt_s, da_s, ddt_s, tot_s,
):
    pair = pl.program_id(0)
    cont = (1 - first_ref[2 * pair + 1]).astype(F32)
    row = lax.broadcasted_iota(jnp.int32, (PAIR, LANES), 0)
    lane = lax.broadcasted_iota(jnp.int32, (PAIR, LANES), 1)
    low_half = lane < HEAD_DIM
    low_g = low_half[:GROUP]
    place = jnp.where(row >= GROUP, row - GROUP, row)
    open_row = jnp.where(row >= GROUP, cont, 0.0)
    tri_t = lax.broadcasted_iota(jnp.int32, (GROUP, GROUP), 0)
    tri_s = lax.broadcasted_iota(jnp.int32, (GROUP, GROUP), 1)
    causal = tri_s <= tri_t

    @pl.when(pair == 0)
    def _():
        dcw_ref[...] = jnp.zeros_like(dcw_ref)
        dcb_ref[...] = jnp.zeros_like(dcb_ref)
        dgg_ref[...] = jnp.zeros_like(dgg_ref)
        dskip_ref[...] = jnp.zeros_like(dskip_ref)
        dhead_ref[...] = jnp.zeros_like(dhead_ref)

    def keep(lag):
        return jnp.where(place >= lag, 1.0, open_row)

    row1 = lax.broadcasted_iota(jnp.int32, (PAIR, 1), 0)
    limit = jnp.where(row1 >= GROUP, len_ref[2 * pair + 1], len_ref[2 * pair])
    live = jnp.where(jnp.where(row1 >= GROUP, row1 - GROUP, row1) < limit, 1.0, 0.0)

    picked = (cot_ref[...].astype(F32) * live).astype(BF16)
    for piece in range(4):
        part = pl.ds(piece * 384, 384)
        dg_s[:, part] = mm(picked, outw_ref[part, :], NT)

    biased = raw_ref[...] + heads_ref[2:3, :]
    small = jnp.exp(-jnp.abs(biased))
    step = jnp.maximum(biased, 0.0) + jnp.where(small < 1e-3, small * (1.0 - 0.5 * small), jnp.log(1.0 + small))
    rate = -jnp.exp(heads_ref[0:1, :])
    log_decay = step * rate
    lower = jnp.where(causal, 1.0, 0.0)
    upper = jnp.where(tri_s >= tri_t, 1.0, 0.0)
    for g in range(2):
        rows = slice(g * GROUP, (g + 1) * GROUP)
        run_s[rows, :] = exact(lower, log_decay[rows]) * LOG2E
    dt_s[...] = step
    at_s[...] = run_s[...].T

    def taps(columns):
        return cw_ref[:, columns], cb_ref[:, columns]

    def conv(j):
        cin = proj_ref[:, pl.ds(pl.multiple_of(INNER + j * LANES, LANES), LANES)]
        columns = pl.ds(pl.multiple_of(j * LANES, LANES), LANES)
        weight, bias = taps(columns)
        mixed = bias + cin * weight[KERNEL - 1 : KERNEL]
        for lag in range(1, KERNEL):
            mixed = mixed + weight[KERNEL - 1 - lag : KERNEL - lag] * (pltpu.roll(cin, lag, 0) * keep(lag))
        m_s[:, columns] = mixed
        return (mixed / (1.0 + jnp.exp(-mixed))).astype(BF16)

    def conv_back(j, grad):
        columns = pl.ds(pl.multiple_of(j * LANES, LANES), LANES)
        place_in = pl.ds(pl.multiple_of(INNER + j * LANES, LANES), LANES)
        weight, _ = taps(columns)
        mixed = m_s[:, columns]
        cin = proj_ref[:, place_in]
        sig = 1.0 / (1.0 + jnp.exp(-mixed))
        dm = grad * (sig * (1.0 + mixed * (1.0 - sig)))
        dcb_ref[:, columns] += jnp.sum(dm, axis=0, keepdims=True)
        total = dm * weight[KERNEL - 1 : KERNEL]
        dws = [jnp.sum(dm * cin, axis=0, keepdims=True)]
        for lag in range(1, KERNEL):
            kept = dm * keep(lag)
            dws.append(jnp.sum(kept * pltpu.roll(cin, lag, 0), axis=0, keepdims=True))
            total = total + pltpu.roll(kept, PAIR - lag, 0) * weight[KERNEL - 1 - lag : KERNEL - lag]
        dcw_ref[:, columns] += jnp.concatenate(dws[::-1], axis=0)
        dproj_ref[:, place_in] = total.astype(BF16)

    b_s[...] = conv(CHUNKS)
    c_s[...] = conv(CHUNKS + 1)
    for g in range(2):
        rows = slice(g * GROUP, (g + 1) * GROUP)
        s_s[g] = jnp.where(causal, mm(c_s[rows, :], b_s[rows, :], NT), 0.0)
        ds_s[g] = jnp.zeros((GROUP, GROUP), F32)
    db_s[...] = jnp.zeros_like(db_s)
    dc_s[...] = jnp.zeros_like(dc_s)
    da_s[...] = jnp.zeros_like(da_s)
    ddt_s[...] = jnp.zeros_like(ddt_s)
    tot_s[...] = jnp.zeros_like(tot_s)

    def column(table, h):
        return jnp.sum(jnp.where(lane == h, table, 0.0), axis=1, keepdims=True)

    def head_columns(hp):
        run, dt = run_s[...], dt_s[...]
        runs = (column(run, 2 * hp), column(run, 2 * hp + 1))
        dts = jnp.where(low_half, column(dt, 2 * hp), column(dt, 2 * hp + 1))
        return runs, jnp.where(low_half, runs[0], runs[1]), dts

    def decay(runs, hp, g, k):
        rows = slice(g * GROUP, (g + 1) * GROUP)
        across = at_s[pl.ds(2 * hp + k, 1), rows]
        return jnp.exp2(jnp.minimum(runs[k][rows] - across, 0.0))

    def to_end(wide):
        return jnp.exp2(wide[GROUP - 1 : GROUP] - wide[:GROUP])

    def forward(hp, sums):
        square, cross = sums
        columns = pl.ds(pl.multiple_of(hp * LANES, LANES), LANES)
        x_low = conv(hp)
        x_s[:, columns] = x_low
        x = x_low.astype(F32)
        runs, wide, dts = head_columns(hp)
        xdt = (x * dts).astype(BF16)
        weighted = (x[:GROUP] * (to_end(wide) * dts[:GROUP])).astype(BF16)
        start = (mm(b_s[:GROUP, :], weighted, TN) * cont).astype(BF16)
        start_s[:, columns] = start
        inner = []
        for g in range(2):
            rows = slice(g * GROUP, (g + 1) * GROUP)
            halves = [mm((s_s[g] * decay(runs, hp, g, k)).astype(BF16), xdt[rows]) for k in range(2)]
            inner.append(jnp.where(low_g, halves[0], halves[1]))
        inner[1] = inner[1] + jnp.exp2(wide[GROUP:]) * mm(c_s[GROUP:, :], start)
        y = jnp.concatenate(inner, axis=0)
        y_s[:, columns] = y
        gate = proj_ref[:, columns]
        gated = (y + skip_ref[:, columns] * x) * (gate / (1.0 + jnp.exp(-gate)))
        return (square + gated * gated, cross + dg_s[:, columns] * gg_ref[:, columns] * gated)

    zero = jnp.zeros((PAIR, LANES), F32)
    square, cross = lax.fori_loop(0, CHUNKS, forward, (zero, zero))
    scale = lax.rsqrt(jnp.sum(square, axis=1, keepdims=True) * (1.0 / INNER) + EPSILON)
    pull = scale * scale * scale * (jnp.sum(cross, axis=1, keepdims=True) * (1.0 / INNER))

    def put(h, value):
        return jnp.where(lane[: value.shape[0]] == h, value, 0.0)

    def head_sums(hp, value):
        first = jnp.sum(jnp.where(low_half[: value.shape[0]], value, 0.0), axis=1, keepdims=True)
        second = jnp.sum(jnp.where(low_half[: value.shape[0]], 0.0, value), axis=1, keepdims=True)
        return put(2 * hp, first) + put(2 * hp + 1, second)

    def backward(hp, carry):
        columns = pl.ds(pl.multiple_of(hp * LANES, LANES), LANES)
        x = x_s[:, columns].astype(F32)
        y = y_s[:, columns]
        skip = skip_ref[:, columns]
        mixer = y + skip * x
        gate = proj_ref[:, columns]
        sig = 1.0 / (1.0 + jnp.exp(-gate))
        act = gate * sig
        gated = mixer * act
        gain = gg_ref[:, columns]
        dgn = dg_s[:, columns]
        unit = gated * scale
        gn_ref[:, columns] = (unit * gain).astype(BF16)
        dgg_ref[:, columns] += jnp.sum(dgn * unit, axis=0, keepdims=True)
        dgated = dgn * gain * scale - gated * pull
        dproj_ref[:, columns] = (dgated * mixer * (sig * (1.0 + gate * (1.0 - sig)))).astype(BF16)
        dy = dgated * act
        dskip_ref[:, columns] += jnp.sum(dy * x, axis=0, keepdims=True)
        dy_low = dy.astype(BF16)
        dyr = dy_low.astype(F32)
        runs, wide, dts = head_columns(hp)
        xdt = (x * dts).astype(BF16)
        dxdt = []
        for g in range(2):
            rows = slice(g * GROUP, (g + 1) * GROUP)
            parts = []
            extra = jnp.zeros((GROUP, GROUP), F32)
            dy_g = dy_low[rows]
            for k in range(2):
                fade = decay(runs, hp, g, k)
                parts.append(mm((s_s[g] * fade).astype(BF16), dy_g, TN))
                mine = jnp.where(low_g if k == 0 else ~low_g, dyr[rows], 0.0).astype(BF16)
                extra = extra + mm(mine, xdt[rows], NT) * fade
            ds_s[g] += extra
            dxdt.append(jnp.where(low_g, parts[0], parts[1]))
        dxdt = jnp.concatenate(dxdt, axis=0)
        start = start_s[:, columns]
        lifted = (dyr[GROUP:] * jnp.exp2(wide[GROUP:])).astype(BF16)
        dc_s[GROUP:, :] += mm(lifted, start, NT)
        dstate = (mm(c_s[GROUP:, :], lifted, TN) * cont).astype(BF16)
        fade_end = to_end(wide)
        weight_end = fade_end * dts[:GROUP]
        weighted = (x[:GROUP] * weight_end).astype(BF16)
        db_s[:GROUP, :] += mm(weighted, dstate, NT)
        dweighted = mm(b_s[:GROUP, :], dstate)
        through = x[:GROUP] * dweighted
        spent = through * weight_end
        da = dyr * y - xdt.astype(F32) * dxdt
        ddt = x * dxdt
        da = jnp.concatenate([da[:GROUP] - spent, da[GROUP:]], axis=0)
        ddt = jnp.concatenate([ddt[:GROUP] + through * fade_end, ddt[GROUP:]], axis=0)
        da_s[...] += head_sums(hp, da)
        ddt_s[...] += head_sums(hp, ddt)
        tot_s[...] += head_sums(hp, jnp.broadcast_to(jnp.sum(spent, axis=0, keepdims=True), (8, LANES)))
        dx = dy * skip + dxdt * dts
        dx = jnp.concatenate([dx[:GROUP] + dweighted * weight_end, dx[GROUP:]], axis=0)
        conv_back(hp, dx)
        return carry

    lax.fori_loop(0, CHUNKS, backward, 0)

    for g in range(2):
        rows = slice(g * GROUP, (g + 1) * GROUP)
        dscore = jnp.where(causal, ds_s[g], 0.0).astype(BF16)
        dc_s[rows, :] += mm(dscore, b_s[rows, :])
        db_s[rows, :] += mm(dscore, c_s[rows, :], TN)
    conv_back(CHUNKS, db_s[...])
    conv_back(CHUNKS + 1, dc_s[...])

    dlog = []
    for g in range(2):
        rows = slice(g * GROUP, (g + 1) * GROUP)
        part = exact(upper, da_s[rows, :])
        dlog.append(part + tot_s[0:1, :] if g == 0 else part)
    dlog = jnp.concatenate(dlog, axis=0)
    step = dt_s[...]
    dstep = ddt_s[...] + dlog * rate
    draw = dstep / (1.0 + jnp.exp(-biased))
    dproj_ref[:, PROJ - HEADS : PROJ] = draw[:, :HEADS].astype(BF16)
    dhead_ref[0:1, :] += jnp.sum(dlog * step, axis=0, keepdims=True) * rate
    dhead_ref[2:3, :] += jnp.sum(draw, axis=0, keepdims=True)

    branch = mm(gn_ref[...], outw_ref[...])
    blk_ref[...] = (tok_ref[...].astype(F32) + live * branch).astype(BF16)


def run_pairs(lengths, firsts, projected, raw, tokens, cotangent, out_w, cw, cb, gg, heads, skip):
    rows = tokens.shape[0]

    def rowwise(width):
        return pl.BlockSpec((PAIR, width), lambda i: (i, 0))

    smem = pl.BlockSpec(memory_space=pltpu.SMEM)
    whole = pl.BlockSpec(memory_space=pltpu.VMEM)
    shape = jax.ShapeDtypeStruct
    return pl.pallas_call(
        pair_kernel,
        grid=(rows // PAIR,),
        in_specs=[smem, smem, rowwise(PROJ), rowwise(LANES), rowwise(D), rowwise(D)] + [whole] * 6,
        out_specs=[rowwise(D), rowwise(INNER), rowwise(PROJ)] + [whole] * 5,
        out_shape=[
            shape((rows, D), BF16),
            shape((rows, INNER), BF16),
            shape((rows, PROJ), BF16),
            shape((KERNEL, CONV_CH), F32),
            shape((1, CONV_CH), F32),
            shape((1, INNER), F32),
            shape((1, INNER), F32),
            shape((8, LANES), F32),
        ],
        scratch_shapes=[
            pltpu.VMEM((PAIR, INNER), F32),
            pltpu.VMEM((PAIR, INNER), F32),
            pltpu.VMEM((PAIR, CONV_CH), F32),
            pltpu.VMEM((PAIR, INNER), BF16),
            pltpu.VMEM((PAIR, LANES), BF16),
            pltpu.VMEM((PAIR, LANES), BF16),
            pltpu.VMEM((STATE, INNER), BF16),
            pltpu.VMEM((2, GROUP, GROUP), F32),
            pltpu.VMEM((2, GROUP, GROUP), F32),
            pltpu.VMEM((PAIR, LANES), F32),
            pltpu.VMEM((PAIR, LANES), F32),
            pltpu.VMEM((LANES, PAIR), F32),
            pltpu.VMEM((PAIR, LANES), F32),
            pltpu.VMEM((PAIR, LANES), F32),
            pltpu.VMEM((PAIR, LANES), F32),
            pltpu.VMEM((PAIR, LANES), F32),
            pltpu.VMEM((8, LANES), F32),
        ],
        compiler_params=pltpu.CompilerParams(
            dimension_semantics=("arbitrary",), vmem_limit_bytes=60 * 1024 * 1024
        ),
    )(lengths, firsts, projected, raw, tokens, cotangent, out_w, cw, cb, gg, heads, skip)


def partners(count, bit):
    return [(i, i ^ (1 << bit)) for i in range(count)]


def own_bit(bit):
    return lax.rem(lax.div(lax.axis_index("dev"), 1 << bit), 2)


def bit_orders(count):
    bits = list(range(count.bit_length() - 1))
    swapped = [bits[0], bits[2], bits[1]] + bits[3:] if len(bits) > 2 else bits
    return bits, swapped


def gather_blocks(block, count, order):
    held = []
    for bit in order[::-1]:
        other = lax.ppermute(block, "dev", partners(count, bit))
        mine = own_bit(bit) == 1
        axis = sum(1 for done in held if done > bit)
        block = jnp.stack([jnp.where(mine, other, block), jnp.where(mine, block, other)], axis=axis)
        held.append(bit)
    return block.reshape((count,) + block.shape[len(held) :])


def scatter_sums(blocks, count, order, sent):
    left = list(range(count.bit_length() - 1))[::-1]
    blocks = blocks.reshape((2,) * len(left) + blocks.shape[1:])
    for bit in order:
        axis = left.index(bit)
        mine = own_bit(bit)
        away = lax.dynamic_index_in_dim(blocks, 1 - mine, axis, keepdims=False).astype(sent)
        kept = lax.dynamic_index_in_dim(blocks, mine, axis, keepdims=False)
        blocks = kept + lax.ppermute(away, "dev", partners(count, bit)).astype(F32)
        left.remove(bit)
    return blocks


def sum_all(value, count):
    for bit in range(count.bit_length() - 1):
        value = value + lax.ppermute(value, "dev", partners(count, bit))
    return value


def body(
    tokens,
    cotangent,
    in_weight,
    out_weight,
    conv_weight,
    conv_bias,
    norm_gain,
    gated_gain,
    head_params,
    group_length,
    group_first,
):
    sizes = (conv_weight.size, conv_bias.size, norm_gain.size, gated_gain.size)
    cuts = (sizes[0], sizes[0] + sizes[1], sizes[0] + sizes[1] + sizes[2])
    ndev = lax.axis_size("dev")
    plain, swapped = bit_orders(ndev)
    owned, width = in_weight.shape
    upper = (owned // 3) * 2
    packed = jnp.concatenate([conv_weight.reshape(-1), conv_bias, norm_gain, gated_gain])
    extra = -(-packed.size // (owned - upper))
    packed = jnp.pad(packed, (0, extra * (owned - upper) - packed.size)).reshape(owned - upper, extra)
    first_rows = gather_blocks(in_weight[:upper], ndev, plain)
    last_rows = gather_blocks(jnp.concatenate([in_weight[upper:], packed], axis=1), ndev, swapped)
    out_w = gather_blocks(out_weight, ndev, swapped).reshape(INNER, D)
    in_w = jnp.concatenate([first_rows, last_rows[:, :, :width]], axis=1).reshape(D, width)
    packed = last_rows[:, :, width:].reshape(ndev, -1)[:, : cuts[2] + sizes[3]].astype(F32)
    conv_w, conv_b, norm_g, gated_g = jnp.split(packed, cuts, axis=1)
    conv_w = conv_w.reshape(CONV_CH, KERNEL).T
    conv_b, norm_g, gated_g = conv_b.reshape(1, -1), norm_g.reshape(1, -1), gated_g.reshape(1, -1)

    token_float = tokens.astype(F32)
    inv = lax.rsqrt(jnp.mean(token_float * token_float, axis=1, keepdims=True) + EPSILON)
    normed_low = (token_float * inv * norm_g).astype(BF16)
    projected = jnp.dot(normed_low, in_w, preferred_element_type=F32)
    raw = jnp.pad(projected[:, PROJ - HEADS :], ((0, 0), (0, LANES - HEADS)))
    heads = jnp.pad(head_params, ((0, 5), (0, LANES - HEADS)))
    skip = jnp.repeat(head_params[1], HEAD_DIM)[None, :]
    block_out, gnormed_low, grad_proj, dcw, dcb, dgg, dskip, dhead = run_pairs(
        group_length, group_first, projected, raw, tokens, cotangent, out_w, conv_w, conv_b, gated_g, heads, skip
    )

    rows = tokens.shape[0]
    slot_place = jnp.arange(rows, dtype=jnp.int32) % GROUP
    live_mask = (slot_place < jnp.repeat(group_length, GROUP)).astype(BF16)[:, None]
    picked = cotangent * live_mask
    out_grad = jnp.dot(gnormed_low.T, picked, preferred_element_type=F32)
    out_grad = scatter_sums(out_grad.reshape((ndev,) + out_weight.shape), ndev, swapped, BF16)
    in_grad = jnp.dot(normed_low.T, grad_proj, preferred_element_type=F32)
    in_grad = in_grad.reshape(ndev, owned, width)
    in_grad = jnp.concatenate(
        [
            scatter_sums(in_grad[:, :upper], ndev, plain, BF16),
            scatter_sums(in_grad[:, upper:], ndev, swapped, BF16),
        ],
        axis=0,
    )
    grad_normed = jnp.dot(grad_proj, in_w.T, preferred_element_type=F32)
    unit = token_float * inv
    grad_norm_g = jnp.sum(grad_normed * unit, axis=0)
    scaled = grad_normed * norm_g
    grad_tokens = inv * (scaled - unit * jnp.mean(scaled * unit, axis=1, keepdims=True))
    token_grad = cotangent.astype(F32) + grad_tokens

    small = jnp.concatenate(
        [
            dcw.T.reshape(ndev, -1),
            dcb.reshape(ndev, -1),
            grad_norm_g.reshape(ndev, -1),
            dgg.reshape(ndev, -1),
        ],
        axis=1,
    )
    head_part = jnp.stack([dhead[0, :HEADS], jnp.sum(dskip.reshape(HEADS, HEAD_DIM), axis=1), dhead[2, :HEADS]])
    head_total = sum_all(head_part, ndev)
    mine = scatter_sums(small, ndev, plain, F32)
    cw_o, cb_o, ng_o, gg_o = jnp.split(mine, cuts)
    return (
        block_out,
        token_grad,
        in_grad,
        out_grad,
        cw_o.reshape(conv_weight.shape),
        cb_o,
        ng_o,
        gg_o,
        head_total,
    )


def solution(mesh):
    placed = (
        P("dev", None),
        P("dev", None),
        P("dev", None),
        P("dev", None),
        P("dev", None),
        P("dev"),
        P("dev"),
        P("dev"),
        P(),
        P("dev"),
        P("dev"),
    )
    return jax.shard_map(
        body,
        mesh=mesh,
        in_specs=placed,
        out_specs=(
            P("dev", None),
            P("dev", None),
            P("dev", None),
            P("dev", None),
            P("dev", None),
            P("dev"),
            P("dev"),
            P("dev"),
            P(),
        ),
        check_vma=False,
    )
```
